256 devices in a mesh: context: 32 (over y_hi, z, core), tensor: 8 (over y_lo, x).
Axes of the slice: x: 4, y: 4 (y_hi: 2, y_lo: 2; y = y_hi * 2 + y_lo), z: 8, core: 2. Of those that a mesh axis runs over, the one named last changes fastest.
Arguments:
- gate_proj: bfloat16 [8192, 8192], P('context', 'tensor'), may hold values from -5 to 5
- key_proj: bfloat16 [8192, 8192], P('context', 'tensor'), may hold values from -5 to 5
- value_proj: bfloat16 [8192, 8192], P('context', 'tensor'), may hold values from -5 to 5
- filters: bfloat16 [8192, 128], P('tensor'), may hold values from -0.5 to 0.5
- residual_in: bfloat16 [8192, 8192], P('context', 'tensor'), may hold values from -55 to 55
- norm_gain: float32 [8192], P('tensor'), may hold values from 0.5 to 1.5
- queries: bfloat16 [8192, 4096], P('context', 'tensor'), may hold values from -22 to 22
- attn_keys: bfloat16 [8192, 4096], P('context', 'tensor'), may hold values from -22 to 22
- attn_values: bfloat16 [8192, 4096], P('context', 'tensor'), may hold values from -5 to 5
Outputs:
- residual_out: bfloat16 [8192, 8192], P('context', 'tensor')
- normed: bfloat16 [8192, 8192], P('context', 'tensor')
- heads_out: bfloat16 [8192, 4096], P('context', 'tensor')
The draws below stay inside these ranges and needn't reach their ends.
All inputs are finite; a program needn't handle non-finite values.
Results may differ from the reference program's by a relative error of at most 0.0065.
Values may be sent and summed in bfloat16 or wider, within the bound.
No kernel may reach another device: no remote copies, remote signals or barrier semaphores. Data moves between devices by JAX's collectives and lax.ppermute only.
A program may use at most 128 MiB of HBM per device.

```python
import math
import jax
import jax.numpy as jnp
from jax import lax

D = 8192
DH = 128
HEADS = 32
TAPS = 128
SEQ = 8192


def draw_queries(key, part):
    key = jax.random.fold_in(key, 3)
    return jnp.clip(jax.random.normal(key, (SEQ, HEADS * DH), jnp.float32), -4.0, 4.0).astype(jnp.bfloat16)


def draw_attn_keys(key, part):
    key = jax.random.fold_in(key, 5)
    return jnp.clip(jax.random.normal(key, (SEQ, HEADS * DH), jnp.float32), -4.0, 4.0).astype(jnp.bfloat16)


def draw_residual_in(key, part):
    key = jax.random.fold_in(key, 7)
    first, second, third = jax.random.split(key, 3)
    channel = jnp.arange(D, dtype=jnp.float32)[None, :] / D
    rough = jax.random.uniform(first, (1, D), jnp.float32, 0.7, 1.4)
    row_scale = 3.0 ** jax.random.uniform(third, (SEQ, 1), jnp.float32, 0.0, 1.0)
    values = jnp.clip(jax.random.normal(second, (SEQ, D), jnp.float32), -4.0, 4.0)
    return (0.8 * 3.0 ** channel * rough * row_scale * values).astype(jnp.bfloat16)


def block_levels(key, shape, shards, smallest, top_value):
    factor_of = 1.0
    for dim, blocks in shards:
        draws = jax.random.uniform(jax.random.fold_in(jax.random.fold_in(key, 6), dim), (blocks,), jnp.float32, smallest / len(shards), top_value / len(shards))
        factor_of = factor_of * jnp.repeat(jnp.exp(draws), shape[dim] // blocks).reshape((-1,) + (1,) * (len(shape) - 1 - dim))
    return factor_of


def centred(key, dims, deviation, bound, cuts=(), kind=jnp.bfloat16):
    values = deviation * jax.random.normal(key, dims, jnp.float32)
    if cuts:
        values = values * block_levels(key, dims, cuts, -0.22, 0.18)
    return jnp.clip(values, -bound, bound).astype(kind)


def setup_inputs(seed: int = 0) -> dict:
    streams_of = jax.random.split(jax.random.key(seed), 10)
    return {
        "gate_proj": centred(streams_of[0], (SEQ, D), 1.0, 5.0, ((0, 32), (1, 8))),
        "key_proj": centred(streams_of[1], (SEQ, D), 1.0, 5.0, ((0, 32), (1, 8))),
        "value_proj": centred(streams_of[2], (SEQ, D), 1.0, 5.0, ((0, 32), (1, 8))),
        "filters": centred(streams_of[3], (D, TAPS), TAPS ** -0.5, 0.5, ((0, 8),)),
        "residual_in": draw_residual_in(jax.random.fold_in(streams_of[9], 71), 0),
        "norm_gain": jnp.clip(1.0 + 0.1 * jax.random.normal(streams_of[5], (D,), jnp.float32), 0.5, 1.5),
        "queries": draw_queries(jax.random.fold_in(streams_of[9], 71), 0),
        "attn_keys": draw_attn_keys(jax.random.fold_in(streams_of[9], 71), 0),
        "attn_values": centred(streams_of[8], (SEQ, HEADS * DH), 1.0, 5.0, ((0, 32), (1, 8))),
    }


def filter_group(operands):
    gated_group, taps_group = operands
    length = taps_group.shape[1]
    row_count = gated_group.shape[0]
    padded = jnp.concatenate([jnp.zeros((length - 1, gated_group.shape[1]), jnp.float32), gated_group.astype(jnp.float32)], axis=0)
    taps = taps_group.astype(jnp.float32)

    def add_tap(offset, running):
        window = lax.dynamic_slice_in_dim(padded, length - 1 - offset, row_count, 0)
        column = lax.dynamic_index_in_dim(taps, offset, 1, keepdims=False)
        return running + window * column[None, :]
    return lax.fori_loop(jnp.int32(0), jnp.int32(length), add_tap, jnp.zeros((row_count, gated_group.shape[1]), jnp.float32))

def attend_head(operands):
    query_head, key_head, value_head = operands
    block = 512
    count = SEQ // block
    scale = 1.0 / math.sqrt(DH)

    def one_block(query_block):
        query_rows = lax.dynamic_slice_in_dim(query_head, query_block * block, block, 0)
        query_pos = query_block * block + jnp.arange(block, dtype=jnp.int32)

        def score_step(key_block, scores):
            key_rows = lax.dynamic_slice_in_dim(key_head, key_block * block, block, 0)
            key_pos = key_block * block + jnp.arange(block, dtype=jnp.int32)
            local = jnp.dot(query_rows, key_rows.T, preferred_element_type=jnp.float32) * scale
            local = jnp.where(key_pos[None, :] <= query_pos[:, None], local, -1e+30)
            return lax.dynamic_update_slice_in_dim(scores, local, key_block * block, 1)
        scores = lax.fori_loop(jnp.int32(0), query_block + 1, score_step, jnp.full((block, SEQ), -1e+30, jnp.float32))
        highest = lax.optimization_barrier(jnp.max(scores, axis=1, keepdims=True))
        weights = jnp.where(scores > -1e+29, jnp.exp(scores - highest), 0.0).astype(jnp.bfloat16)
        totals = lax.optimization_barrier(jnp.sum(weights.astype(jnp.float32), axis=1, keepdims=True))

        def value_step(key_block, running):
            weight_rows = lax.dynamic_slice_in_dim(weights, key_block * block, block, 1)
            value_rows = lax.dynamic_slice_in_dim(value_head, key_block * block, block, 0)
            return running + jnp.dot(weight_rows, value_rows, preferred_element_type=jnp.float32)
        summed = lax.fori_loop(jnp.int32(0), query_block + 1, value_step, jnp.zeros((block, value_head.shape[1]), jnp.float32))
        return (summed / totals).astype(jnp.bfloat16)
    blocks = lax.map(one_block, jnp.arange(count, dtype=jnp.int32))
    return blocks.reshape(SEQ, value_head.shape[1])

def reference(gate_proj, key_proj, value_proj, filters, residual_in, norm_gain, queries, attn_keys, attn_values):
    gated = (key_proj.astype(jnp.float32) * value_proj.astype(jnp.float32)).astype(jnp.bfloat16)
    group = math.gcd(D, 512)
    count = D // group
    gated_groups = gated.reshape(SEQ, count, group).transpose(1, 0, 2)
    tap_groups = filters.reshape(count, group, TAPS)
    filtered = lax.map(filter_group, (gated_groups, tap_groups)).transpose(1, 0, 2).reshape(SEQ, D)
    residual_out = (residual_in.astype(jnp.float32) + gate_proj.astype(jnp.float32) * filtered).astype(jnp.bfloat16)
    widened = residual_out.astype(jnp.float32)
    mean_square = lax.optimization_barrier(jnp.mean(widened * widened, axis=1, keepdims=True))
    normed = (widened * lax.rsqrt(mean_square + 1e-06) * norm_gain[None, :]).astype(jnp.bfloat16)
    query_heads = queries.reshape(SEQ, HEADS, DH).transpose(1, 0, 2)
    key_heads = attn_keys.reshape(SEQ, HEADS, DH).transpose(1, 0, 2)
    value_heads = attn_values.reshape(SEQ, HEADS, DH).transpose(1, 0, 2)
    outputs = lax.map(attend_head, (query_heads, key_heads, value_heads))
    heads_out = outputs.transpose(1, 0, 2).reshape(SEQ, HEADS * DH)
    return (residual_out, normed, heads_out)
```

```python
import functools
import math

import jax
import jax.numpy as jnp
import ml_dtypes
import numpy as np
from jax import lax
from jax.experimental import pallas as pl
from jax.experimental.pallas import tpu as pltpu
from jax.sharding import PartitionSpec as P

D = 8192
DH = 128
ROWS = 256
TAPS = 128
SPAN = ROWS + TAPS
ZS = 8
LOG2E_SCALE = math.log2(math.e) / math.sqrt(DH)
LOW = -1e30
F32 = jnp.float32
BF16 = jnp.bfloat16


def pairs(where):
    out = []
    for plane in range(2):
        for z in range(ZS):
            for core in range(2):
                to = where(plane, z, core)
                if to is not None:
                    p, zz, c = to
                    out.append(((plane * ZS + z) * 2 + core, (p * ZS + zz % ZS) * 2 + c))
    return out


def hop(steps):
    return pairs(lambda p, z, c: (p, z + steps[z % 2], c))


NEAR = [None, hop((-1, 1)), hop((2, -2)), hop((-3, 3))]
SIBLING = pairs(lambda p, z, c: (p, z ^ 1, c))
CORE = pairs(lambda p, z, c: (p, z, 1 - c))
DOWN = pairs(lambda p, z, c: (1, z, c) if p == 0 else None)
NEXT = [(i, i + 1) for i in range(2 * ZS * 2 - 1)]


def send(x, where):
    return lax.ppermute(x, "context", where)


def back(x, where):
    return lax.ppermute(x, "context", [(b, a) for a, b in where])


def place():
    index = lax.axis_index("context")
    core = lax.rem(index, 2)
    z = lax.rem(lax.div(index, 2), ZS)
    plane = lax.div(index, 2 * ZS)
    return plane, z, core


def target_heads(z):
    odd = lax.rem(z, 2)
    offsets = [0, -1 + 2 * odd, 2 - 4 * odd, -3 + 6 * odd]
    return [lax.div(lax.rem(z + o + ZS, ZS), 2) for o in offsets]


def pack_kernel(q_ref, k_ref, v_ref, *outs):
    _, z, _ = place()
    for head, out in zip(target_heads(z), outs):
        columns = pl.ds(pl.multiple_of(head * DH, DH), DH)
        out[0:ROWS, :] = q_ref[:, columns]
        out[ROWS : 2 * ROWS, :] = k_ref[:, columns]
        out[2 * ROWS : 3 * ROWS, :] = v_ref[:, columns]


def pack(q, k, v):
    return pl.pallas_call(
        pack_kernel,
        out_shape=[jax.ShapeDtypeStruct((3 * ROWS, DH), BF16)] * 4,
        in_specs=[pl.BlockSpec(memory_space=pltpu.VMEM)] * 3,
        out_specs=[pl.BlockSpec(memory_space=pltpu.VMEM)] * 4,
        compiler_params=pltpu.CompilerParams(vmem_limit_bytes=16 << 20),
        name="pack",
    )(q, k, v)


def unpack_kernel(o0, o1, o2, o3, out):
    _, z, _ = place()
    for head, piece in zip(target_heads(z), (o0, o1, o2, o3)):
        out[:, pl.ds(pl.multiple_of(head * DH, DH), DH)] = piece[...]


def unpack(pieces):
    return pl.pallas_call(
        unpack_kernel,
        out_shape=jax.ShapeDtypeStruct((ROWS, 4 * DH), BF16),
        in_specs=[pl.BlockSpec(memory_space=pltpu.VMEM)] * 4,
        out_specs=pl.BlockSpec(memory_space=pltpu.VMEM),
        compiler_params=pltpu.CompilerParams(vmem_limit_bytes=16 << 20),
        name="unpack",
    )(*pieces)


def wave_kernel(blocks, first, last, count, *refs):
    q_refs = refs[:4]
    array_refs = refs[4 : 4 + count]
    rest = refs[4 + count :]
    if not first:
        acc_in, high_in = rest[:2]
        rest = rest[2:]
    if last:
        outs = rest[:4]
        q_all, acc, high = rest[4:7]
        rest = rest[7:]
    else:
        acc, high = rest[:2]
        q_all = rest[2]
        rest = rest[3:]
    s_all = rest[0]
    plane, z, core = place()
    odd = lax.rem(z, 2)
    sign = 2 * odd - 1
    for j in range(4):
        q_all[j] = q_refs[j][0:ROWS, :]
    if first:
        acc[...] = jnp.zeros_like(acc)
        high[...] = jnp.full_like(high, LOW)
    else:
        acc[...] = acc_in[...]
        high[...] = high_in[...]
    ones = jnp.ones((ROWS, DH), BF16)
    skew = lax.broadcasted_iota(jnp.int32, (ROWS, ROWS), 1) - lax.broadcasted_iota(
        jnp.int32, (ROWS, ROWS), 0
    )

    def source(far, j):
        if far:
            return lax.rem((z + 1 - 2 * odd) - sign * j + ZS, ZS)
        return lax.rem(z + sign * j + ZS, ZS)

    def run(chosen):
        def per_query(i, carry):
            q = q_all[i]
            q_block = 2 * lax.rem(z + sign * i + ZS, ZS) + core
            rows = pl.ds(pl.multiple_of(i * ROWS, ROWS), ROWS)
            old = high[rows, :]
            top = old
            for n, (array, k_row, v_row, lower, far, j, other) in enumerate(chosen):
                keys = array_refs[array][k_row : k_row + ROWS, :]
                s = lax.dot_general(
                    q, keys, (((1,), (1,)), ((), ())), preferred_element_type=F32
                )
                if not lower:
                    k_block = 2 * source(far, j) + (1 - core if other else core)
                    s = jnp.where(skew <= (q_block - k_block) * ROWS, s, LOW)
                s_all[n] = s
                top = jnp.maximum(top, jnp.maximum(s[:, :DH], s[:, DH:]))
            best = jnp.max(top, axis=1, keepdims=True)
            scale = jnp.exp2((old[:, :1] - best) * LOG2E_SCALE)
            total = acc[rows, :] * scale
            for n, (array, k_row, v_row, lower, far, j, other) in enumerate(chosen):
                p = jnp.exp2((s_all[n] - best) * LOG2E_SCALE).astype(BF16)
                values = array_refs[array][v_row : v_row + ROWS, :]
                total = total + jnp.dot(
                    p, jnp.concatenate([values, ones], axis=1), preferred_element_type=F32
                )
            acc[rows, :] = total
            high[rows, :] = jnp.broadcast_to(best, (ROWS, DH))
            return carry

        lax.fori_loop(0, 4, per_query, 0)

    own = [b for b in blocks if not b[3]]
    lower = [b for b in blocks if b[3]]
    if own:
        run(own)
    if lower:

        @pl.when(plane == 1)
        def _():
            run(lower)

    if last:
        for i in range(4):
            part = acc[i * ROWS : (i + 1) * ROWS, :]
            outs[i][...] = (part[:, :DH] / part[:, DH:]).astype(BF16)


def wave(q_arrays, arrays, blocks, state, last=False):
    first = state is None
    most = max(sum(1 for b in blocks if not b[3]), sum(1 for b in blocks if b[3]))
    state_shapes = [((4 * ROWS, 2 * DH), F32), ((4 * ROWS, DH), F32)]
    q_scratch = pltpu.VMEM((4, ROWS, DH), BF16)
    s_scratch = pltpu.VMEM((most, ROWS, ROWS), F32)
    vmem = pl.BlockSpec(memory_space=pltpu.VMEM)
    if last:
        out_shape = [jax.ShapeDtypeStruct((ROWS, DH), BF16)] * 4
        scratch = [q_scratch] + [pltpu.VMEM(s, d) for s, d in state_shapes] + [s_scratch]
    else:
        out_shape = [jax.ShapeDtypeStruct(s, d) for s, d in state_shapes]
        scratch = [q_scratch, s_scratch]
    operands = list(q_arrays) + list(arrays) + ([] if first else list(state))
    tiles = 4 * len(blocks)
    return pl.pallas_call(
        functools.partial(wave_kernel, blocks, first, last, len(arrays)),
        out_shape=out_shape,
        in_specs=[vmem] * len(operands),
        out_specs=[vmem] * len(out_shape),
        scratch_shapes=scratch,
        compiler_params=pltpu.CompilerParams(vmem_limit_bytes=40 << 20),
        cost_estimate=pl.CostEstimate(
            flops=tiles * 4 * ROWS * ROWS * DH,
            bytes_accessed=sum(o.size * o.dtype.itemsize for o in operands),
            transcendentals=tiles * ROWS * ROWS,
        ),
        name="wave",
    )(*operands)


def kv_of(message):
    return message[ROWS:]


def attention(queries, attn_keys, attn_values):
    messages = pack(queries, attn_keys, attn_values)
    got = [messages[0]] + [send(messages[j], NEAR[j]) for j in (1, 2, 3)]
    kv0 = kv_of(got[0])
    far0 = send(kv0, SIBLING)
    low0 = send(kv0, DOWN)
    kv12 = jnp.concatenate([kv_of(got[1]), kv_of(got[2])])
    far12 = send(kv12, SIBLING)
    mid = jnp.concatenate([kv12, far0])
    low12 = send(mid, DOWN)
    core1 = send(jnp.concatenate([kv0, mid]), CORE)
    kv3 = kv_of(got[3])
    far3 = send(kv3, SIBLING)
    late = jnp.concatenate([kv3, far12])
    low3 = send(late, DOWN)
    core2 = send(late, CORE)
    low4 = send(far3, DOWN)
    core3 = send(jnp.concatenate([far3, low0, low12]), CORE)
    core4 = send(jnp.concatenate([low3, low4]), CORE)

    def block(array, first_row, lower, far, j, other):
        return (array, first_row, first_row + ROWS, lower, far, j, other)

    def group(array, spots, lower, other, skip=0):
        return [
            block(array, skip + 2 * ROWS * n, lower, far, j, other)
            for n, (far, j) in enumerate(spots)
        ]

    first = [(False, 0), (False, 1), (False, 2), (True, 0)]
    second = [(False, 3), (True, 1), (True, 2)]
    third = [(True, 3)]
    state = wave(
        got,
        [got[0], got[1], got[2], far0, core1],
        [block(n, ROWS, False, False, n, False) for n in range(3)]
        + group(3, [(True, 0)], False, False)
        + group(4, first, False, True),
        None,
    )
    state = wave(
        got,
        [got[3], far12, core2],
        [block(0, ROWS, False, False, 3, False)]
        + group(1, second[1:], False, False)
        + group(2, second, False, True),
        state,
    )
    state = wave(
        got,
        [far3, core3, low0, low12],
        group(0, third, False, False)
        + group(1, third, False, True)
        + group(1, first, True, True, 2 * ROWS)
        + group(2, first[:1], True, False)
        + group(3, first[1:], True, False),
        state,
    )
    pieces = wave(
        got,
        [low3, low4, core4],
        group(0, second, True, False)
        + group(1, third, True, False)
        + group(2, second + third, True, True),
        state,
        last=True,
    )
    returned = [pieces[0]] + [back(pieces[j], NEAR[j]) for j in (1, 2, 3)]
    return unpack(returned)


def split(x):
    top = x.astype(BF16)
    return top, (x - top.astype(F32)).astype(BF16)


def transform():
    k = np.arange(SPAN // 2)[:, None] + 0.5
    t = np.arange(SPAN)[None, :]
    angle = 2 * np.pi * k * t / SPAN
    forward = np.concatenate([np.cos(angle), np.sin(angle)], axis=0)
    inverse = forward[:, TAPS:].T * (2.0 / SPAN)

    def halves(a):
        top = a.astype(ml_dtypes.bfloat16)
        return [top, (a - top.astype(np.float64)).astype(ml_dtypes.bfloat16)]

    return halves(forward) + halves(inverse)


def filter_kernel(
    fh_ref, fl_ref, gh_ref, gl_ref, key_ref, value_ref, gate_ref, res_ref, taps_ref, halo_ref,
    out_ref, squares_ref,
):
    def dot(a, b):
        return jnp.dot(a, b, preferred_element_type=F32)

    def dot_t(a, b):
        return lax.dot_general(a, b, (((1,), (1,)), ((), ())), preferred_element_type=F32)

    gated = (key_ref[...].astype(F32) * value_ref[...].astype(F32)).astype(BF16)
    x = jnp.concatenate([halo_ref[...], gated], axis=0)
    spectrum = dot(fh_ref[...], x) + dot(fl_ref[...], x)
    taps = taps_ref[...]
    weight = dot_t(fh_ref[:, :TAPS], taps) + dot_t(fl_ref[:, :TAPS], taps)
    half = SPAN // 2
    xc, xs = spectrum[:half], spectrum[half:]
    wc, ws = weight[:half], weight[half:]
    both = jnp.concatenate([xc * wc - xs * ws, xc * ws + xs * wc], axis=0)
    top, low = split(both)
    filtered = dot(gh_ref[...], top) + dot(gh_ref[...], low) + dot(gl_ref[...], top)
    out = (res_ref[...].astype(F32) + gate_ref[...].astype(F32) * filtered).astype(BF16)
    out_ref[...] = out
    wide = out.astype(F32)
    s_top, s_low = split(wide * wide)
    ones = jnp.ones((8, out.shape[1]), BF16)

    @pl.when(pl.program_id(0) == 0)
    def _():
        squares_ref[...] = jnp.zeros_like(squares_ref)

    squares_ref[...] += dot_t(ones, s_top) + dot_t(ones, s_low)


def filter_block(gate, key, value, filters, residual, halo):
    channels = gate.shape[1]
    tile = 256
    rows = pl.BlockSpec((ROWS, tile), lambda i: (0, i))
    whole = lambda a: pl.BlockSpec(a.shape, lambda i: (0, 0))
    matrices = [jnp.asarray(m) for m in transform()]
    return pl.pallas_call(
        filter_kernel,
        grid=(channels // tile,),
        out_shape=[
            jax.ShapeDtypeStruct((ROWS, channels), BF16),
            jax.ShapeDtypeStruct((8, ROWS), F32),
        ],
        in_specs=[whole(m) for m in matrices]
        + [rows] * 4
        + [
            pl.BlockSpec((tile, TAPS), lambda i: (i, 0)),
            pl.BlockSpec((TAPS, tile), lambda i: (0, i)),
        ],
        out_specs=[rows, pl.BlockSpec((8, ROWS), lambda i: (0, 0))],
        compiler_params=pltpu.CompilerParams(vmem_limit_bytes=32 << 20),
        cost_estimate=pl.CostEstimate(
            flops=1500000000, bytes_accessed=5 << 20, transcendentals=0
        ),
        name="filter",
    )(*matrices, key, value, gate, residual, filters, halo)


def sum_over_tensor(x):
    for bit in (1, 2, 4):
        x = x + lax.ppermute(x, "tensor", [(i, i ^ bit) for i in range(8)])
    return x


def local(
    gate_proj,
    key_proj,
    value_proj,
    filters,
    residual_in,
    norm_gain,
    queries,
    attn_keys,
    attn_values,
):
    heads_out = attention(queries, attn_keys, attn_values)
    tail = slice(ROWS - TAPS, ROWS)
    edge = (key_proj[tail].astype(F32) * value_proj[tail].astype(F32)).astype(BF16)
    halo = send(edge, NEXT)
    residual_out, squares = filter_block(
        gate_proj, key_proj, value_proj, filters, residual_in, halo
    )
    mean_square = sum_over_tensor(squares[0])[:, None] / D
    normed = (
        residual_out.astype(F32) * lax.rsqrt(mean_square + 1e-06) * norm_gain[None, :]
    ).astype(BF16)
    return (residual_out, normed, heads_out)


def solution(mesh):
    split_both = P("context", "tensor")
    return jax.shard_map(
        local,
        mesh=mesh,
        in_specs=(
            split_both,
            split_both,
            split_both,
            P("tensor", None),
            split_both,
            P("tensor"),
            split_both,
            split_both,
            split_both,
        ),
        out_specs=(split_both, split_both, split_both),
        check_vma=False,
    )
```

```python
import functools
import math

import jax
import jax.numpy as jnp
import ml_dtypes
import numpy as np
from jax import lax
from jax.experimental import pallas as pl
from jax.experimental.pallas import tpu as pltpu
from jax.sharding import PartitionSpec as P

D = 8192
DH = 128
ROWS = 256
TAPS = 128
SPAN = 2 * TAPS
ZS = 8
LOG2E_SCALE = math.log2(math.e) / math.sqrt(DH)
LOW = -1e30
F32 = jnp.float32
BF16 = jnp.bfloat16


def pairs(where):
    out = []
    for plane in range(2):
        for z in range(ZS):
            for core in range(2):
                to = where(plane, z, core)
                if to is not None:
                    p, zz, c = to
                    out.append(((plane * ZS + z) * 2 + core, (p * ZS + zz % ZS) * 2 + c))
    return out


def hop(steps):
    return pairs(lambda p, z, c: (p, z + steps[z % 2], c))


NEAR = [None, hop((-1, 1)), hop((2, -2)), hop((-3, 3))]
SIBLING = pairs(lambda p, z, c: (p, z ^ 1, c))
CORE = pairs(lambda p, z, c: (p, z, 1 - c))
DOWN = pairs(lambda p, z, c: (1, z, c) if p == 0 else None)
NEXT = [(i, i + 1) for i in range(2 * ZS * 2 - 1)]


def send(x, where):
    return lax.ppermute(x, "context", where)


def back(x, where):
    return lax.ppermute(x, "context", [(b, a) for a, b in where])


def place():
    index = lax.axis_index("context")
    core = lax.rem(index, 2)
    z = lax.rem(lax.div(index, 2), ZS)
    plane = lax.div(index, 2 * ZS)
    return plane, z, core


def target_heads(z):
    odd = lax.rem(z, 2)
    offsets = [0, -1 + 2 * odd, 2 - 4 * odd, -3 + 6 * odd]
    return [lax.div(lax.rem(z + o + ZS, ZS), 2) for o in offsets]


def pack_kernel(
    q_ref, k_ref, v_ref, key_ref, value_ref, edge, o0, o1, o2, o3, own, key_tail, value_tail, sems
):
    _, z, _ = place()
    tails = [
        pltpu.make_async_copy(ref.at[ROWS - TAPS : ROWS, :], tail, sems.at[12 + n])
        for n, (ref, tail) in enumerate(((key_ref, key_tail), (value_ref, value_tail)))
    ]
    copies = []
    for j, (head, out) in enumerate(zip(target_heads(z), (o0, o1, o2, o3))):
        columns = pl.ds(pl.multiple_of(head * DH, DH), DH)
        for n, ref in enumerate((q_ref, k_ref, v_ref)):
            copies.append(
                pltpu.make_async_copy(
                    ref.at[:, columns], out.at[n * ROWS : (n + 1) * ROWS, :], sems.at[3 * j + n]
                )
            )
    columns = pl.ds(pl.multiple_of(target_heads(z)[0] * DH, DH), DH)
    for n, ref in enumerate((k_ref, v_ref)):
        copies.append(
            pltpu.make_async_copy(
                ref.at[:, columns], own.at[n * ROWS : (n + 1) * ROWS, :], sems.at[14 + n]
            )
        )
    for copy in copies + tails:
        copy.start()
    for copy in tails:
        copy.wait()
    edge[...] = (key_tail[...].astype(F32) * value_tail[...].astype(F32)).astype(BF16)
    for copy in copies:
        copy.wait()


def pack(q, k, v, key, value):
    channels = key.shape[1]
    return pl.pallas_call(
        pack_kernel,
        out_shape=[jax.ShapeDtypeStruct((TAPS, channels), BF16)]
        + [jax.ShapeDtypeStruct((3 * ROWS, DH), BF16)] * 4
        + [jax.ShapeDtypeStruct((2 * ROWS, DH), BF16)],
        in_specs=[pl.BlockSpec(memory_space=pltpu.HBM)] * 5,
        out_specs=[pl.BlockSpec(memory_space=pltpu.VMEM)] * 6,
        scratch_shapes=[pltpu.VMEM((TAPS, channels), BF16)] * 2
        + [pltpu.SemaphoreType.DMA((16,))],
        compiler_params=pltpu.CompilerParams(vmem_limit_bytes=60 << 20),
        name="pack",
    )(q, k, v, key, value)


def unpack_kernel(o0, o1, o2, o3, out):
    _, z, _ = place()
    for head, piece in zip(target_heads(z), (o0, o1, o2, o3)):
        out[:, pl.ds(pl.multiple_of(head * DH, DH), DH)] = piece[...]


def unpack(pieces):
    return pl.pallas_call(
        unpack_kernel,
        out_shape=jax.ShapeDtypeStruct((ROWS, 4 * DH), BF16),
        in_specs=[pl.BlockSpec(memory_space=pltpu.VMEM)] * 4,
        out_specs=pl.BlockSpec(memory_space=pltpu.VMEM),
        compiler_params=pltpu.CompilerParams(vmem_limit_bytes=16 << 20),
        name="unpack",
    )(*pieces)


def wave_kernel(blocks, first, last, count, *refs):
    q_refs = refs[:4]
    array_refs = refs[4 : 4 + count]
    rest = refs[4 + count :]
    if not first:
        acc_in, high_in = rest[:2]
        rest = rest[2:]
    if last:
        outs = rest[:4]
        rest = rest[4:]
    else:
        acc, high = rest[:2]
        rest = rest[2:]
    s_all, values_all = rest
    plane, z, core = place()
    odd = lax.rem(z, 2)
    sign = 2 * odd - 1
    skew = lax.broadcasted_iota(jnp.int32, (ROWS, ROWS), 1) - lax.broadcasted_iota(
        jnp.int32, (ROWS, ROWS), 0
    )
    values_all[:, DH:] = jnp.ones((values_all.shape[0], DH), BF16)

    def source(far, j):
        if far:
            return lax.rem((z + 1 - 2 * odd) - sign * j + ZS, ZS)
        return lax.rem(z + sign * j + ZS, ZS)

    def run(chosen):
        width = len(chosen) * ROWS
        for n, (array, k_row, v_row, lower, far, j, other) in enumerate(chosen):
            values_all[n * ROWS : (n + 1) * ROWS, :DH] = array_refs[array][v_row : v_row + ROWS, :]

        def scores(i):
            q = q_refs[i][0:ROWS, :]
            q_block = 2 * lax.rem(z + sign * i + ZS, ZS) + core
            old = None if first else high_in[i * ROWS : (i + 1) * ROWS, :]
            top = old
            for n, (array, k_row, v_row, lower, far, j, other) in enumerate(chosen):
                keys = array_refs[array][k_row : k_row + ROWS, :]
                s = lax.dot_general(
                    q, keys, (((1,), (1,)), ((), ())), preferred_element_type=F32
                )
                if not lower:
                    k_block = 2 * source(far, j) + (1 - core if other else core)
                    s = jnp.where(skew <= (q_block - k_block) * ROWS, s, LOW)
                s_all[i % 2, :, n * ROWS : (n + 1) * ROWS] = s
                pair = jnp.maximum(s[:, :DH], s[:, DH:])
                top = pair if top is None else jnp.maximum(top, pair)
            best = jnp.max(top, axis=1, keepdims=True)
            scale = None if first else jnp.exp2((old[:, :1] - best) * LOG2E_SCALE)
            return best, scale

        def weigh(i, best, scale):
            rows = slice(i * ROWS, (i + 1) * ROWS)
            p = jnp.exp2((s_all[i % 2, :, :width] - best) * LOG2E_SCALE).astype(BF16)
            total = jnp.dot(p, values_all[:width, :], preferred_element_type=F32)
            if not first:
                total = total + acc_in[rows, :] * scale
            if last:
                outs[i][...] = (total[:, :DH] / total[:, DH:]).astype(BF16)
            else:
                acc[rows, :] = total
                high[rows, :] = jnp.broadcast_to(best, (ROWS, DH))

        state = scores(0)
        for i in range(4):
            following = scores(i + 1) if i < 3 else None
            weigh(i, *state)
            state = following

    def keep():
        if last:
            for i in range(4):
                part = acc_in[i * ROWS : (i + 1) * ROWS, :]
                outs[i][...] = (part[:, :DH] / part[:, DH:]).astype(BF16)
        else:
            acc[...] = acc_in[...]
            high[...] = high_in[...]

    own = [b for b in blocks if not b[3]]
    if len(own) == len(blocks):
        run(own)
    else:

        @pl.when(plane == 1)
        def _():
            run(blocks)

        @pl.when(plane == 0)
        def _():
            if own:
                run(own)
            else:
                keep()


SMALL = pl.CostEstimate(flops=1024, bytes_accessed=1024, transcendentals=0)


def wave(q_arrays, arrays, blocks, state, last=False):
    first = state is None
    width = len(blocks) * ROWS
    state_shapes = [((4 * ROWS, 2 * DH), F32), ((4 * ROWS, DH), F32)]
    vmem = pl.BlockSpec(memory_space=pltpu.VMEM)
    if last:
        out_shape = [jax.ShapeDtypeStruct((ROWS, DH), BF16)] * 4
    else:
        out_shape = [jax.ShapeDtypeStruct(s, d) for s, d in state_shapes]
    operands = list(q_arrays) + list(arrays) + ([] if first else list(state))
    tiles = 4 * len(blocks)
    return pl.pallas_call(
        functools.partial(wave_kernel, blocks, first, last, len(arrays)),
        out_shape=out_shape,
        in_specs=[vmem] * len(operands),
        out_specs=[vmem] * len(out_shape),
        scratch_shapes=[
            pltpu.VMEM((2, ROWS, width), F32),
            pltpu.VMEM((width, 2 * DH), BF16),
        ],
        compiler_params=pltpu.CompilerParams(vmem_limit_bytes=32 << 20),
        cost_estimate=SMALL,
        name="wave",
    )(*operands)


def tie(x, *before):
    return lax.optimization_barrier((x,) + before)[0]


def kv_of(message):
    return message[ROWS:]


def tie(x, *before):
    return lax.optimization_barrier((x,) + before)[0]


def block(array, first_row, lower, far, j, other):
    return (array, first_row, first_row + ROWS, lower, far, j, other)


def group(array, spots, lower, other, skip=0):
    return [
        block(array, skip + 2 * ROWS * n, lower, far, j, other) for n, (far, j) in enumerate(spots)
    ]


def split(x):
    top = x.astype(BF16)
    return top, (x - top.astype(F32)).astype(BF16)


def transform():
    k = np.arange(SPAN // 2)[:, None] + 0.5
    t = np.arange(SPAN)[None, :]
    angle = 2 * np.pi * k * t / SPAN
    forward = np.concatenate([np.cos(angle), np.sin(angle)], axis=0)
    inverse = forward[:, TAPS:].T * (2.0 / SPAN)

    def halves(a):
        top = a.astype(ml_dtypes.bfloat16)
        return [top, (a - top.astype(np.float64)).astype(ml_dtypes.bfloat16)]

    return np.concatenate(
        [np.concatenate(halves(forward), axis=1), np.concatenate(halves(inverse), axis=1)], axis=0
    )


def filter_kernel(
    matrix_ref, key_ref, value_ref, gate_ref, res_ref, taps_ref, halo_ref,
    out_ref, squares_ref,
):
    def dot(a, b):
        return jnp.dot(a, b, preferred_element_type=F32)

    def dot_t(a, b):
        return lax.dot_general(a, b, (((1,), (1,)), ((), ())), preferred_element_type=F32)

    half = SPAN // 2
    fh, fl = matrix_ref[:SPAN, :SPAN], matrix_ref[:SPAN, SPAN:]
    gh, gl = matrix_ref[SPAN:, :SPAN], matrix_ref[SPAN:, SPAN:]
    gated = (key_ref[...].astype(F32) * value_ref[...].astype(F32)).astype(BF16)
    width = gated.shape[1]
    x = jnp.concatenate(
        [jnp.concatenate([halo_ref[...], gated[:TAPS]], axis=0), gated], axis=1
    )
    spectrum = dot(fh, x) + dot(fl, x)
    taps = taps_ref[...]
    weight = dot_t(fh[:, :TAPS], taps) + dot_t(fl[:, :TAPS], taps)
    xc, xs = spectrum[:half], spectrum[half:]
    wc, ws = [jnp.concatenate([w, w], axis=1) for w in (weight[:half], weight[half:])]
    both = jnp.concatenate([xc * wc - xs * ws, xc * ws + xs * wc], axis=0)
    top, low = split(both)
    filtered = dot(gh, top) + dot(gh, low) + dot(gl, top)
    filtered = jnp.concatenate([filtered[:, :width], filtered[:, width:]], axis=0)
    out = (res_ref[...].astype(F32) + gate_ref[...].astype(F32) * filtered).astype(BF16)
    out_ref[...] = out
    wide = out.astype(F32)
    s_top, s_low = split(wide * wide)
    ones = jnp.ones((8, out.shape[1]), BF16)

    @pl.when(pl.program_id(0) == 0)
    def _():
        squares_ref[...] = jnp.zeros_like(squares_ref)

    squares_ref[...] += dot_t(ones, s_top) + dot_t(ones, s_low)


def filter_block(gate, key, value, filters, residual, halo):
    channels = gate.shape[1]
    tile = 256
    rows = pl.BlockSpec((ROWS, tile), lambda i: (0, i))
    whole = lambda a: pl.BlockSpec(a.shape, lambda i: (0, 0))
    matrix = jnp.asarray(transform())
    return pl.pallas_call(
        filter_kernel,
        grid=(channels // tile,),
        out_shape=[
            jax.ShapeDtypeStruct((ROWS, channels), BF16),
            jax.ShapeDtypeStruct((8, ROWS), F32),
        ],
        in_specs=[whole(matrix)]
        + [rows] * 4
        + [
            pl.BlockSpec((tile, TAPS), lambda i: (i, 0)),
            pl.BlockSpec((TAPS, tile), lambda i: (0, i)),
        ],
        out_specs=[rows, pl.BlockSpec((8, ROWS), lambda i: (0, 0))],
        compiler_params=pltpu.CompilerParams(vmem_limit_bytes=32 << 20),
        cost_estimate=SMALL,
        name="filter",
    )(matrix, key, value, gate, residual, filters, halo)


def swap_sum(x, bit):
    return x + lax.ppermute(x, "tensor", [(i, i ^ bit) for i in range(8)])


def local(
    gate_proj,
    key_proj,
    value_proj,
    filters,
    residual_in,
    norm_gain,
    queries,
    attn_keys,
    attn_values,
):
    edge, *messages, kv0 = pack(queries, attn_keys, attn_values, key_proj, value_proj)
    one = send(messages[1], NEAR[1])
    two = send(messages[2], NEAR[2])
    far0 = send(kv0, SIBLING)
    low0 = send(kv0, DOWN)
    halo = send(edge, NEXT)

    three = send(tie(messages[3], one), NEAR[3])
    kv12 = tie(jnp.concatenate([kv_of(one), kv_of(two)]), far0, low0)
    far12 = send(kv12, SIBLING)
    mid = jnp.concatenate([kv12, far0])
    low12 = send(mid, DOWN)
    core1 = send(jnp.concatenate([kv0, mid]), CORE)

    gate_proj, key_proj, value_proj, filters, residual_in, _ = lax.optimization_barrier(
        (gate_proj, key_proj, value_proj, filters, residual_in, messages[0])
    )
    residual_out, squares = filter_block(
        gate_proj, key_proj, value_proj, filters, residual_in, tie(halo, kv12)
    )
    total = swap_sum(squares[0], 1)

    kv3 = tie(kv_of(three), squares)
    far3 = send(kv3, SIBLING)
    late = jnp.concatenate([kv3, far12])
    low3 = send(late, DOWN)
    core2 = send(late, CORE)
    got = [messages[0], one, two, three]
    first = [(False, 0), (False, 1), (False, 2), (True, 0)]
    second = [(False, 3), (True, 1), (True, 2)]
    third = [(True, 3)]
    state = wave(
        got,
        [got[0], got[1], got[2], far0, core1],
        [block(n, ROWS, False, False, n, False) for n in range(3)]
        + group(3, [(True, 0)], False, False)
        + group(4, first, False, True),
        None,
    )
    far3 = tie(far3, state[1])
    low4 = send(far3, DOWN)
    core3 = send(jnp.concatenate([far3, low0, low12]), CORE)
    total = swap_sum(total, 2)
    state = wave(
        got,
        [got[3], far12, tie(core2, total)],
        [block(0, ROWS, False, False, 3, False)]
        + group(1, second[1:], False, False)
        + group(2, second, False, True),
        state,
    )
    low3 = tie(low3, state[1])
    core4 = send(jnp.concatenate([low3, low4]), CORE)
    total = swap_sum(total, 4)
    state = wave(
        got,
        [far3, tie(core3, total), low0, low12],
        group(0, third, False, False)
        + group(1, third, False, True)
        + group(1, first, True, True, 2 * ROWS)
        + group(2, first[:1], True, False)
        + group(3, first[1:], True, False),
        state,
    )
    pieces = wave(
        got,
        [low3, low4, core4],
        group(0, second, True, False)
        + group(1, third, True, False)
        + group(2, second + third, True, True),
        state,
        last=True,
    )
    returning = [back(pieces[j], NEAR[j]) for j in (3, 2, 1)]
    returned = [pieces[0]] + returning[::-1]
    heads_out = unpack(returned)

    mean_square = total[:, None] / D
    normed = (
        residual_out.astype(F32) * lax.rsqrt(mean_square + 1e-06) * norm_gain[None, :]
    ).astype(BF16)
    return (residual_out, normed, heads_out)


def solution(mesh):
    split_both = P("context", "tensor")
    return jax.shard_map(
        local,
        mesh=mesh,
        in_specs=(
            split_both,
            split_both,
            split_both,
            P("tensor", None),
            split_both,
            P("tensor"),
            split_both,
            split_both,
            split_both,
        ),
        out_specs=(split_both, split_both, split_both),
        check_vma=False,
    )
```

```python
import functools
import math

import jax
import jax.numpy as jnp
import ml_dtypes
import numpy as np
from jax import lax
from jax.experimental import pallas as pl
from jax.experimental.pallas import tpu as pltpu
from jax.sharding import PartitionSpec as P

D = 8192
DH = 128
ROWS = 256
TAPS = 128
SPAN = 2 * TAPS
ZS = 8
LOG2E_SCALE = math.log2(math.e) / math.sqrt(DH)
LOW = -1e30
F32 = jnp.float32
BF16 = jnp.bfloat16


def pairs(where):
    out = []
    for plane in range(2):
        for z in range(ZS):
            for core in range(2):
                to = where(plane, z, core)
                if to is not None:
                    p, zz, c = to
                    out.append(((plane * ZS + z) * 2 + core, (p * ZS + zz % ZS) * 2 + c))
    return out


def hop(steps):
    return pairs(lambda p, z, c: (p, z + steps[z % 2], c))


NEAR = [None, hop((-1, 1)), hop((2, -2)), hop((-3, 3))]
SIBLING = pairs(lambda p, z, c: (p, z ^ 1, c))
CORE = pairs(lambda p, z, c: (p, z, 1 - c))
DOWN = pairs(lambda p, z, c: (1, z, c) if p == 0 else None)
NEXT = [(i, i + 1) for i in range(2 * ZS * 2 - 1)]


def send(x, where):
    return lax.ppermute(x, "context", where)


def back(x, where):
    return lax.ppermute(x, "context", [(b, a) for a, b in where])


def place():
    index = lax.axis_index("context")
    core = lax.rem(index, 2)
    z = lax.rem(lax.div(index, 2), ZS)
    plane = lax.div(index, 2 * ZS)
    return plane, z, core


def target_heads(z):
    odd = lax.rem(z, 2)
    offsets = [0, -1 + 2 * odd, 2 - 4 * odd, -3 + 6 * odd]
    return [lax.div(lax.rem(z + o + ZS, ZS), 2) for o in offsets]


def pack_kernel(
    q_ref, k_ref, v_ref, key_ref, value_ref, edge, o0, o1, o2, o3, own, key_tail, value_tail, sems
):
    _, z, _ = place()
    tails = [
        pltpu.make_async_copy(ref.at[ROWS - TAPS : ROWS, :], tail, sems.at[12 + n])
        for n, (ref, tail) in enumerate(((key_ref, key_tail), (value_ref, value_tail)))
    ]
    copies = []
    for j, (head, out) in enumerate(zip(target_heads(z), (o0, o1, o2, o3))):
        columns = pl.ds(pl.multiple_of(head * DH, DH), DH)
        for n, ref in enumerate((q_ref, k_ref, v_ref)):
            copies.append(
                pltpu.make_async_copy(
                    ref.at[:, columns], out.at[n * ROWS : (n + 1) * ROWS, :], sems.at[3 * j + n]
                )
            )
    columns = pl.ds(pl.multiple_of(target_heads(z)[0] * DH, DH), DH)
    for n, ref in enumerate((k_ref, v_ref)):
        copies.append(
            pltpu.make_async_copy(
                ref.at[:, columns], own.at[n * ROWS : (n + 1) * ROWS, :], sems.at[14 + n]
            )
        )
    for copy in copies + tails:
        copy.start()
    for copy in tails:
        copy.wait()
    edge[...] = (key_tail[...].astype(F32) * value_tail[...].astype(F32)).astype(BF16)
    for copy in copies:
        copy.wait()


def pack(q, k, v, key, value):
    channels = key.shape[1]
    return pl.pallas_call(
        pack_kernel,
        out_shape=[jax.ShapeDtypeStruct((TAPS, channels), BF16)]
        + [jax.ShapeDtypeStruct((3 * ROWS, DH), BF16)] * 4
        + [jax.ShapeDtypeStruct((2 * ROWS, DH), BF16)],
        in_specs=[pl.BlockSpec(memory_space=pltpu.HBM)] * 5,
        out_specs=[pl.BlockSpec(memory_space=pltpu.VMEM)] * 6,
        scratch_shapes=[pltpu.VMEM((TAPS, channels), BF16)] * 2
        + [pltpu.SemaphoreType.DMA((16,))],
        compiler_params=pltpu.CompilerParams(vmem_limit_bytes=60 << 20),
        name="pack",
    )(q, k, v, key, value)


def unpack_kernel(o0, o1, o2, o3, out):
    _, z, _ = place()
    for head, piece in zip(target_heads(z), (o0, o1, o2, o3)):
        out[:, pl.ds(pl.multiple_of(head * DH, DH), DH)] = piece[...]


def unpack(pieces):
    return pl.pallas_call(
        unpack_kernel,
        out_shape=jax.ShapeDtypeStruct((ROWS, 4 * DH), BF16),
        in_specs=[pl.BlockSpec(memory_space=pltpu.VMEM)] * 4,
        out_specs=pl.BlockSpec(memory_space=pltpu.VMEM),
        compiler_params=pltpu.CompilerParams(vmem_limit_bytes=16 << 20),
        name="unpack",
    )(*pieces)


def wave_kernel(blocks, first, last, count, *refs):
    q_refs = refs[:4]
    array_refs = refs[4 : 4 + count]
    rest = refs[4 + count :]
    if not first:
        acc_in, high_in = rest[:2]
        rest = rest[2:]
    if last:
        outs = rest[:4]
        rest = rest[4:]
    else:
        acc, high = rest[:2]
        rest = rest[2:]
    s_all, values_all = rest
    plane, z, core = place()
    odd = lax.rem(z, 2)
    sign = 2 * odd - 1
    skew = lax.broadcasted_iota(jnp.int32, (ROWS, ROWS), 1) - lax.broadcasted_iota(
        jnp.int32, (ROWS, ROWS), 0
    )
    values_all[:, DH:] = jnp.ones((values_all.shape[0], DH), BF16)

    def source(far, j):
        if far:
            return lax.rem((z + 1 - 2 * odd) - sign * j + ZS, ZS)
        return lax.rem(z + sign * j + ZS, ZS)

    def run(chosen):
        width = len(chosen) * ROWS
        for n, (array, k_row, v_row, lower, far, j, other) in enumerate(chosen):
            values_all[n * ROWS : (n + 1) * ROWS, :DH] = array_refs[array][v_row : v_row + ROWS, :]

        def scores(i):
            q = q_refs[i][0:ROWS, :]
            q_block = 2 * lax.rem(z + sign * i + ZS, ZS) + core
            old = None if first else high_in[i * ROWS : (i + 1) * ROWS, :]
            top = old
            for n, (array, k_row, v_row, lower, far, j, other) in enumerate(chosen):
                keys = array_refs[array][k_row : k_row + ROWS, :]
                s = lax.dot_general(
                    q, keys, (((1,), (1,)), ((), ())), preferred_element_type=F32
                )
                if not lower:
                    k_block = 2 * source(far, j) + (1 - core if other else core)
                    s = jnp.where(skew <= (q_block - k_block) * ROWS, s, LOW)
                s_all[i % 2, :, n * ROWS : (n + 1) * ROWS] = s
                pair = jnp.maximum(s[:, :DH], s[:, DH:])
                top = pair if top is None else jnp.maximum(top, pair)
            best = jnp.max(top, axis=1, keepdims=True)
            scale = None if first else jnp.exp2((old[:, :1] - best) * LOG2E_SCALE)
            return best, scale

        def weigh(i, best, scale):
            rows = slice(i * ROWS, (i + 1) * ROWS)
            p = jnp.exp2((s_all[i % 2, :, :width] - best) * LOG2E_SCALE).astype(BF16)
            total = jnp.dot(p, values_all[:width, :], preferred_element_type=F32)
            if not first:
                total = total + acc_in[rows, :] * scale
            if last:
                outs[i][...] = (total[:, :DH] / total[:, DH:]).astype(BF16)
            else:
                acc[rows, :] = total
                high[rows, :] = jnp.broadcast_to(best, (ROWS, DH))

        state = scores(0)
        for i in range(4):
            following = scores(i + 1) if i < 3 else None
            weigh(i, *state)
            state = following

    def keep():
        if last:
            for i in range(4):
                part = acc_in[i * ROWS : (i + 1) * ROWS, :]
                outs[i][...] = (part[:, :DH] / part[:, DH:]).astype(BF16)
        else:
            acc[...] = acc_in[...]
            high[...] = high_in[...]

    own = [b for b in blocks if not b[3]]
    if len(own) == len(blocks):
        run(own)
    else:

        @pl.when(plane == 1)
        def _():
            run(blocks)

        @pl.when(plane == 0)
        def _():
            if own:
                run(own)
            else:
                keep()


SMALL = pl.CostEstimate(flops=1024, bytes_accessed=1024, transcendentals=0)


def wave(q_arrays, arrays, blocks, state, last=False):
    first = state is None
    width = len(blocks) * ROWS
    state_shapes = [((4 * ROWS, 2 * DH), F32), ((4 * ROWS, DH), F32)]
    vmem = pl.BlockSpec(memory_space=pltpu.VMEM)
    if last:
        out_shape = [jax.ShapeDtypeStruct((ROWS, DH), BF16)] * 4
    else:
        out_shape = [jax.ShapeDtypeStruct(s, d) for s, d in state_shapes]
    operands = list(q_arrays) + list(arrays) + ([] if first else list(state))
    tiles = 4 * len(blocks)
    return pl.pallas_call(
        functools.partial(wave_kernel, blocks, first, last, len(arrays)),
        out_shape=out_shape,
        in_specs=[vmem] * len(operands),
        out_specs=[vmem] * len(out_shape),
        scratch_shapes=[
            pltpu.VMEM((2, ROWS, width), F32),
            pltpu.VMEM((width, 2 * DH), BF16),
        ],
        compiler_params=pltpu.CompilerParams(vmem_limit_bytes=32 << 20),
        cost_estimate=SMALL,
        name="wave",
    )(*operands)


def tie(x, *before):
    return lax.optimization_barrier((x,) + before)[0]


def kv_of(message):
    return message[ROWS:]


def tie(x, *before):
    return lax.optimization_barrier((x,) + before)[0]


def block(array, first_row, lower, far, j, other):
    return (array, first_row, first_row + ROWS, lower, far, j, other)


def group(array, spots, lower, other, skip=0):
    return [
        block(array, skip + 2 * ROWS * n, lower, far, j, other) for n, (far, j) in enumerate(spots)
    ]


def split(x):
    top = x.astype(BF16)
    return top, (x - top.astype(F32)).astype(BF16)


def transform():
    k = np.arange(SPAN // 2)[:, None] + 0.5
    t = np.arange(SPAN)[None, :]
    angle = 2 * np.pi * k * t / SPAN
    forward = np.concatenate([np.cos(angle), np.sin(angle)], axis=0)
    inverse = forward[:, TAPS:].T * (2.0 / SPAN)

    def halves(a):
        top = a.astype(ml_dtypes.bfloat16)
        return [top, (a - top.astype(np.float64)).astype(ml_dtypes.bfloat16)]

    return np.concatenate(
        [np.concatenate(halves(forward), axis=1), np.concatenate(halves(inverse), axis=1)], axis=0
    )


def filter_kernel(
    tile, matrix_ref, key_ref, value_ref, gate_ref, res_ref, taps_ref, halo_ref, out_ref, squares_ref
):
    def dot(a, b):
        return jnp.dot(a, b, preferred_element_type=F32)

    def dot_t(a, b):
        return lax.dot_general(a, b, (((1,), (1,)), ((), ())), preferred_element_type=F32)

    half = SPAN // 2
    fh, fl = matrix_ref[:SPAN, :SPAN], matrix_ref[:SPAN, SPAN:]
    gh, gl = matrix_ref[SPAN:, :SPAN], matrix_ref[SPAN:, SPAN:]
    ones = jnp.ones((8, tile), BF16)
    squares = jnp.zeros((8, ROWS), F32)
    for first in range(0, key_ref.shape[1], tile):
        columns = slice(first, first + tile)
        gated = (key_ref[:, columns].astype(F32) * value_ref[:, columns].astype(F32)).astype(BF16)
        x = jnp.concatenate(
            [jnp.concatenate([halo_ref[:, columns], gated[:TAPS]], axis=0), gated], axis=1
        )
        spectrum = dot(fh, x) + dot(fl, x)
        taps = taps_ref[columns, :]
        weight = dot_t(fh[:, :TAPS], taps) + dot_t(fl[:, :TAPS], taps)
        xc, xs = spectrum[:half], spectrum[half:]
        wc, ws = [jnp.concatenate([w, w], axis=1) for w in (weight[:half], weight[half:])]
        both = jnp.concatenate([xc * wc - xs * ws, xc * ws + xs * wc], axis=0)
        top, low = split(both)
        filtered = dot(gh, top) + dot(gh, low) + dot(gl, top)
        filtered = jnp.concatenate([filtered[:, :tile], filtered[:, tile:]], axis=0)
        out = (
            res_ref[:, columns].astype(F32) + gate_ref[:, columns].astype(F32) * filtered
        ).astype(BF16)
        out_ref[:, columns] = out
        wide = out.astype(F32)
        s_top, s_low = split(wide * wide)
        squares = squares + dot_t(ones, s_top) + dot_t(ones, s_low)
    squares_ref[...] = squares


def filter_block(gate, key, value, filters, residual, halo):
    channels = gate.shape[1]
    vmem = pl.BlockSpec(memory_space=pltpu.VMEM)
    return pl.pallas_call(
        functools.partial(filter_kernel, 256),
        out_shape=[
            jax.ShapeDtypeStruct((ROWS, channels), BF16),
            jax.ShapeDtypeStruct((8, ROWS), F32),
        ],
        in_specs=[vmem] * 7,
        out_specs=[vmem] * 2,
        compiler_params=pltpu.CompilerParams(vmem_limit_bytes=32 << 20),
        cost_estimate=SMALL,
        name="filter",
    )(jnp.asarray(transform()), key, value, gate, residual, filters, halo)


def swap_sum(x, bit, *before):
    return lax.ppermute(x, "tensor", [(i, i ^ bit) for i in range(8)]) + tie(x, *before)


def local(
    gate_proj,
    key_proj,
    value_proj,
    filters,
    residual_in,
    norm_gain,
    queries,
    attn_keys,
    attn_values,
):
    edge, *messages, kv0 = pack(queries, attn_keys, attn_values, key_proj, value_proj)
    one = send(messages[1], NEAR[1])
    two = send(messages[2], NEAR[2])
    far0 = send(kv0, SIBLING)
    low0 = send(kv0, DOWN)
    halo = send(edge, NEXT)

    three = send(tie(messages[3], one), NEAR[3])
    kv12 = tie(jnp.concatenate([kv_of(one), kv_of(two)]), far0, low0)
    far12 = send(kv12, SIBLING)
    mid = jnp.concatenate([kv12, far0])
    low12 = send(mid, DOWN)
    core1 = send(jnp.concatenate([kv0, mid]), CORE)

    gate_proj, key_proj, value_proj, filters, residual_in, _ = lax.optimization_barrier(
        (gate_proj, key_proj, value_proj, filters, residual_in, messages[0])
    )
    residual_out, squares = filter_block(
        gate_proj, key_proj, value_proj, filters, residual_in, tie(halo, kv12)
    )
    kv3 = tie(kv_of(three), squares)
    far3 = send(kv3, SIBLING)
    total = swap_sum(squares[0], 1, kv3)
    late = jnp.concatenate([kv3, far12])
    low3 = send(late, DOWN)
    core2 = send(late, CORE)
    got = [messages[0], one, two, three]
    first = [(False, 0), (False, 1), (False, 2), (True, 0)]
    second = [(False, 3), (True, 1), (True, 2)]
    third = [(True, 3)]
    state = wave(
        got,
        [got[0], got[1], got[2], far0, core1],
        [block(n, ROWS, False, False, n, False) for n in range(3)]
        + group(3, [(True, 0)], False, False)
        + group(4, first, False, True),
        None,
    )
    far3 = tie(far3, state[1])
    low4 = send(far3, DOWN)
    core3 = send(jnp.concatenate([far3, low0, low12]), CORE)
    total = swap_sum(total, 2, state[1])
    state = wave(
        got,
        [got[3], far12, tie(core2, total), far3, low0, low12],
        [block(0, ROWS, False, False, 3, False)]
        + group(1, second[1:], False, False)
        + group(2, second, False, True)
        + group(3, third, False, False)
        + group(4, first[:1], True, False)
        + group(5, first[1:], True, False),
        state,
    )
    low3 = tie(low3, state[1])
    core4 = send(jnp.concatenate([low3, low4]), CORE)
    state = wave(
        got,
        [core3],
        group(0, third, False, True) + group(0, first, True, True, 2 * ROWS),
        state,
    )
    pieces = wave(
        got,
        [low3, low4, core4],
        group(0, second, True, False)
        + group(1, third, True, False)
        + group(2, second + third, True, True),
        state,
        last=True,
    )
    total = swap_sum(total, 4, pieces[0])
    returning = [back(pieces[j], NEAR[j]) for j in (3, 2, 1)]
    returned = [pieces[0]] + returning[::-1]
    heads_out = unpack(returned)

    mean_square = total[:, None] / D
    normed = (
        residual_out.astype(F32) * lax.rsqrt(mean_square + 1e-06) * norm_gain[None, :]
    ).astype(BF16)
    return (residual_out, normed, heads_out)


def solution(mesh):
    split_both = P("context", "tensor")
    return jax.shard_map(
        local,
        mesh=mesh,
        in_specs=(
            split_both,
            split_both,
            split_both,
            P("tensor", None),
            split_both,
            P("tensor"),
            split_both,
            split_both,
            split_both,
        ),
        out_specs=(split_both, split_both, split_both),
        check_vma=False,
    )
```

```python
import functools
import math

import jax
import jax.numpy as jnp
import ml_dtypes
import numpy as np
from jax import lax
from jax.experimental import pallas as pl
from jax.experimental.pallas import tpu as pltpu
from jax.sharding import PartitionSpec as P

D = 8192
DH = 128
ROWS = 256
TAPS = 128
SPAN = 2 * TAPS
ZS = 8
LOG2E_SCALE = math.log2(math.e) / math.sqrt(DH)
LOW = -1e30
F32 = jnp.float32
BF16 = jnp.bfloat16


def pairs(where):
    out = []
    for plane in range(2):
        for z in range(ZS):
            for core in range(2):
                to = where(plane, z, core)
                if to is not None:
                    p, zz, c = to
                    out.append(((plane * ZS + z) * 2 + core, (p * ZS + zz % ZS) * 2 + c))
    return out


def hop(steps):
    return pairs(lambda p, z, c: (p, z + steps[z % 2], c))


NEAR = [None, hop((-1, 1)), hop((2, -2)), hop((-3, 3))]
SIBLING = pairs(lambda p, z, c: (p, z ^ 1, c))
CORE = pairs(lambda p, z, c: (p, z, 1 - c))
DOWN = pairs(lambda p, z, c: (1, z, c) if p == 0 else None)
ASLANT = pairs(lambda p, z, c: (1, z ^ 1, c) if p == 0 else None)
NEXT = [(i, i + 1) for i in range(2 * ZS * 2 - 1)]


def send(x, where):
    return lax.ppermute(x, "context", where)


def back(x, where):
    return lax.ppermute(x, "context", [(b, a) for a, b in where])


def place():
    index = lax.axis_index("context")
    core = lax.rem(index, 2)
    z = lax.rem(lax.div(index, 2), ZS)
    plane = lax.div(index, 2 * ZS)
    return plane, z, core


def target_heads(z):
    odd = lax.rem(z, 2)
    offsets = [0, -1 + 2 * odd, 2 - 4 * odd, -3 + 6 * odd]
    return [lax.div(lax.rem(z + o + ZS, ZS), 2) for o in offsets]


def column_copies(refs, out, head, sems):
    columns = pl.ds(pl.multiple_of(head * DH, DH), DH)
    return [
        pltpu.make_async_copy(ref.at[:, columns], out.at[n * ROWS : (n + 1) * ROWS, :], sems.at[n])
        for n, ref in enumerate(refs)
    ]


def pack_kernel(q_ref, k_ref, v_ref, o1, o2, sems):
    heads = target_heads(place()[1])
    copies = []
    for n, (j, out) in enumerate(((1, o1), (2, o2))):
        copies += column_copies((q_ref, k_ref, v_ref), out, heads[j], sems.at[n])
    for copy in copies:
        copy.start()
    for copy in copies:
        copy.wait()


def pack_rest_kernel(
    q_ref, k_ref, v_ref, key_ref, value_ref, edge, o0, o3, own, key_tail, value_tail, sems
):
    heads = target_heads(place()[1])
    tails = [
        pltpu.make_async_copy(ref.at[ROWS - TAPS : ROWS, :], tail, sems.at[3, n])
        for n, (ref, tail) in enumerate(((key_ref, key_tail), (value_ref, value_tail)))
    ]
    copies = column_copies((k_ref, v_ref), own, heads[0], sems.at[0])
    for n, (j, out) in enumerate(((0, o0), (3, o3))):
        copies += column_copies((q_ref, k_ref, v_ref), out, heads[j], sems.at[1 + n])
    for copy in copies + tails:
        copy.start()
    for copy in tails:
        copy.wait()
    edge[...] = (key_tail[...].astype(F32) * value_tail[...].astype(F32)).astype(BF16)
    for copy in copies:
        copy.wait()


def pack(q, k, v):
    return pl.pallas_call(
        pack_kernel,
        out_shape=[jax.ShapeDtypeStruct((3 * ROWS, DH), BF16)] * 2,
        in_specs=[pl.BlockSpec(memory_space=pltpu.HBM)] * 3,
        out_specs=[pl.BlockSpec(memory_space=pltpu.VMEM)] * 2,
        scratch_shapes=[pltpu.SemaphoreType.DMA((2, 3))],
        compiler_params=pltpu.CompilerParams(vmem_limit_bytes=60 << 20),
        name="pack",
    )(q, k, v)


def pack_rest(q, k, v, key, value):
    channels = key.shape[1]
    return pl.pallas_call(
        pack_rest_kernel,
        out_shape=[jax.ShapeDtypeStruct((TAPS, channels), BF16)]
        + [jax.ShapeDtypeStruct((3 * ROWS, DH), BF16)] * 2
        + [jax.ShapeDtypeStruct((2 * ROWS, DH), BF16)],
        in_specs=[pl.BlockSpec(memory_space=pltpu.HBM)] * 5,
        out_specs=[pl.BlockSpec(memory_space=pltpu.VMEM)] * 4,
        scratch_shapes=[pltpu.VMEM((TAPS, channels), BF16)] * 2
        + [pltpu.SemaphoreType.DMA((4, 3))],
        compiler_params=pltpu.CompilerParams(vmem_limit_bytes=60 << 20),
        name="pack_rest",
    )(q, k, v, key, value)


def unpack_kernel(o0, o1, o2, o3, out):
    _, z, _ = place()
    for head, piece in zip(target_heads(z), (o0, o1, o2, o3)):
        out[:, pl.ds(pl.multiple_of(head * DH, DH), DH)] = piece[...]


def unpack(pieces):
    return pl.pallas_call(
        unpack_kernel,
        out_shape=jax.ShapeDtypeStruct((ROWS, 4 * DH), BF16),
        in_specs=[pl.BlockSpec(memory_space=pltpu.VMEM)] * 4,
        out_specs=pl.BlockSpec(memory_space=pltpu.VMEM),
        compiler_params=pltpu.CompilerParams(vmem_limit_bytes=16 << 20),
        name="unpack",
    )(*pieces)


def wave_kernel(blocks, first, last, count, *refs):
    q_refs = refs[:4]
    array_refs = refs[4 : 4 + count]
    rest = refs[4 + count :]
    if not first:
        acc_in, high_in = rest[:2]
        rest = rest[2:]
    if last:
        outs = rest[:4]
        rest = rest[4:]
    else:
        acc, high = rest[:2]
        rest = rest[2:]
    s_all, values_all = rest
    plane, z, core = place()
    odd = lax.rem(z, 2)
    sign = 2 * odd - 1
    skew = lax.broadcasted_iota(jnp.int32, (ROWS, ROWS), 1) - lax.broadcasted_iota(
        jnp.int32, (ROWS, ROWS), 0
    )
    values_all[:, DH:] = jnp.ones((values_all.shape[0], DH), BF16)

    def source(far, j):
        if far:
            return lax.rem((z + 1 - 2 * odd) - sign * j + ZS, ZS)
        return lax.rem(z + sign * j + ZS, ZS)

    def run(chosen):
        width = len(chosen) * ROWS
        for n, (array, k_row, v_row, lower, far, j, other) in enumerate(chosen):
            values_all[n * ROWS : (n + 1) * ROWS, :DH] = array_refs[array][v_row : v_row + ROWS, :]

        def scores(i):
            q = q_refs[i][0:ROWS, :]
            q_block = 2 * lax.rem(z + sign * i + ZS, ZS) + core
            old = None if first else high_in[i * ROWS : (i + 1) * ROWS, :]
            top = old
            for n, (array, k_row, v_row, lower, far, j, other) in enumerate(chosen):
                keys = array_refs[array][k_row : k_row + ROWS, :]
                s = lax.dot_general(
                    q, keys, (((1,), (1,)), ((), ())), preferred_element_type=F32
                )
                if not lower:
                    k_block = 2 * source(far, j) + (1 - core if other else core)
                    s = jnp.where(skew <= (q_block - k_block) * ROWS, s, LOW)
                s_all[i % 2, :, n * ROWS : (n + 1) * ROWS] = s
                pair = jnp.maximum(s[:, :DH], s[:, DH:])
                top = pair if top is None else jnp.maximum(top, pair)
            best = jnp.max(top, axis=1, keepdims=True)
            scale = None if first else jnp.exp2((old[:, :1] - best) * LOG2E_SCALE)
            return best, scale

        def weigh(i, best, scale):
            rows = slice(i * ROWS, (i + 1) * ROWS)
            p = jnp.exp2((s_all[i % 2, :, :width] - best) * LOG2E_SCALE).astype(BF16)
            total = jnp.dot(p, values_all[:width, :], preferred_element_type=F32)
            if not first:
                total = total + acc_in[rows, :] * scale
            if last:
                outs[i][...] = (total[:, :DH] / total[:, DH:]).astype(BF16)
            else:
                acc[rows, :] = total
                high[rows, :] = jnp.broadcast_to(best, (ROWS, DH))

        state = scores(0)
        for i in range(4):
            following = scores(i + 1) if i < 3 else None
            weigh(i, *state)
            state = following

    def keep():
        if last:
            for i in range(4):
                part = acc_in[i * ROWS : (i + 1) * ROWS, :]
                outs[i][...] = (part[:, :DH] / part[:, DH:]).astype(BF16)
        else:
            acc[...] = acc_in[...]
            high[...] = high_in[...]

    own = [b for b in blocks if not b[3]]
    if len(own) == len(blocks):
        run(own)
    else:

        @pl.when(plane == 1)
        def _():
            run(blocks)

        @pl.when(plane == 0)
        def _():
            if own:
                run(own)
            else:
                keep()


SMALL = pl.CostEstimate(flops=1024, bytes_accessed=1024, transcendentals=0)


def wave(q_arrays, arrays, blocks, state, last=False):
    first = state is None
    width = len(blocks) * ROWS
    state_shapes = [((4 * ROWS, 2 * DH), F32), ((4 * ROWS, DH), F32)]
    vmem = pl.BlockSpec(memory_space=pltpu.VMEM)
    if last:
        out_shape = [jax.ShapeDtypeStruct((ROWS, DH), BF16)] * 4
    else:
        out_shape = [jax.ShapeDtypeStruct(s, d) for s, d in state_shapes]
    operands = list(q_arrays) + list(arrays) + ([] if first else list(state))
    tiles = 4 * len(blocks)
    return pl.pallas_call(
        functools.partial(wave_kernel, blocks, first, last, len(arrays)),
        out_shape=out_shape,
        in_specs=[vmem] * len(operands),
        out_specs=[vmem] * len(out_shape),
        scratch_shapes=[
            pltpu.VMEM((2, ROWS, width), F32),
            pltpu.VMEM((width, 2 * DH), BF16),
        ],
        compiler_params=pltpu.CompilerParams(vmem_limit_bytes=32 << 20),
        cost_estimate=SMALL,
        name="wave",
    )(*operands)


def tie(x, *before):
    return lax.optimization_barrier((x,) + before)[0]


def kv_of(message):
    return message[ROWS:]


def tie(x, *before):
    return lax.optimization_barrier((x,) + before)[0]


def block(array, first_row, lower, far, j, other):
    return (array, first_row, first_row + ROWS, lower, far, j, other)


def group(array, spots, lower, other, skip=0):
    return [
        block(array, skip + 2 * ROWS * n, lower, far, j, other) for n, (far, j) in enumerate(spots)
    ]


def split(x):
    top = x.astype(BF16)
    return top, (x - top.astype(F32)).astype(BF16)


def transform():
    k = np.arange(SPAN // 2)[:, None] + 0.5
    t = np.arange(SPAN)[None, :]
    angle = 2 * np.pi * k * t / SPAN
    forward = np.concatenate([np.cos(angle), np.sin(angle)], axis=0)
    inverse = forward[:, TAPS:].T * (2.0 / SPAN)

    def halves(a):
        top = a.astype(ml_dtypes.bfloat16)
        return [top, (a - top.astype(np.float64)).astype(ml_dtypes.bfloat16)]

    return np.concatenate(
        [np.concatenate(halves(forward), axis=1), np.concatenate(halves(inverse), axis=1)], axis=0
    )


def filter_kernel(
    tile, matrix_ref, key_ref, value_ref, gate_ref, res_ref, taps_ref, halo_ref, out_ref, squares_ref
):
    def dot(a, b):
        return jnp.dot(a, b, preferred_element_type=F32)

    def dot_t(a, b):
        return lax.dot_general(a, b, (((1,), (1,)), ((), ())), preferred_element_type=F32)

    half = SPAN // 2
    fh, fl = matrix_ref[:SPAN, :SPAN], matrix_ref[:SPAN, SPAN:]
    gh, gl = matrix_ref[SPAN:, :SPAN], matrix_ref[SPAN:, SPAN:]
    ones = jnp.ones((8, tile), BF16)
    squares = jnp.zeros((8, ROWS), F32)
    for first in range(0, key_ref.shape[1], tile):
        columns = slice(first, first + tile)
        gated = (key_ref[:, columns].astype(F32) * value_ref[:, columns].astype(F32)).astype(BF16)
        x = jnp.concatenate(
            [jnp.concatenate([halo_ref[:, columns], gated[:TAPS]], axis=0), gated], axis=1
        )
        spectrum = dot(fh, x) + dot(fl, x)
        taps = taps_ref[columns, :]
        weight = dot_t(fh[:, :TAPS], taps) + dot_t(fl[:, :TAPS], taps)
        xc, xs = spectrum[:half], spectrum[half:]
        wc, ws = [jnp.concatenate([w, w], axis=1) for w in (weight[:half], weight[half:])]
        both = jnp.concatenate([xc * wc - xs * ws, xc * ws + xs * wc], axis=0)
        top, low = split(both)
        filtered = dot(gh, top) + dot(gh, low) + dot(gl, top)
        filtered = jnp.concatenate([filtered[:, :tile], filtered[:, tile:]], axis=0)
        out = (
            res_ref[:, columns].astype(F32) + gate_ref[:, columns].astype(F32) * filtered
        ).astype(BF16)
        out_ref[:, columns] = out
        wide = out.astype(F32)
        s_top, s_low = split(wide * wide)
        squares = squares + dot_t(ones, s_top) + dot_t(ones, s_low)
    squares_ref[...] = squares


def filter_block(gate, key, value, filters, residual, halo):
    channels = gate.shape[1]
    vmem = pl.BlockSpec(memory_space=pltpu.VMEM)
    return pl.pallas_call(
        functools.partial(filter_kernel, 256),
        out_shape=[
            jax.ShapeDtypeStruct((ROWS, channels), BF16),
            jax.ShapeDtypeStruct((8, ROWS), F32),
        ],
        in_specs=[vmem] * 7,
        out_specs=[vmem] * 2,
        compiler_params=pltpu.CompilerParams(vmem_limit_bytes=32 << 20),
        cost_estimate=SMALL,
        name="filter",
    )(jnp.asarray(transform()), key, value, gate, residual, filters, halo)


def swap_sum(x, bit, *before):
    return lax.ppermute(x, "tensor", [(i, i ^ bit) for i in range(8)]) + tie(x, *before)


def local(
    gate_proj,
    key_proj,
    value_proj,
    filters,
    residual_in,
    norm_gain,
    queries,
    attn_keys,
    attn_values,
):
    message1, message2 = pack(queries, attn_keys, attn_values)
    one = send(message1, NEAR[1])
    two = send(message2, NEAR[2])
    edge, message0, message3, kv0 = pack_rest(
        tie(queries, message1), attn_keys, attn_values, key_proj, value_proj
    )
    messages = [message0, message1, message2, message3]
    far0 = send(kv0, SIBLING)
    low0 = send(kv0, DOWN)
    halo = send(edge, NEXT)

    three = send(tie(messages[3], one), NEAR[3])
    kv12 = tie(jnp.concatenate([kv_of(one), kv_of(two)]), far0, low0)
    far12 = send(kv12, SIBLING)
    mid = jnp.concatenate([kv12, far0])
    low12 = send(mid, DOWN)
    core1 = send(jnp.concatenate([kv0, mid]), CORE)

    gate_proj, key_proj, value_proj, filters, residual_in, _ = lax.optimization_barrier(
        (gate_proj, key_proj, value_proj, filters, residual_in, messages[0])
    )
    residual_out, squares = filter_block(
        gate_proj, key_proj, value_proj, filters, residual_in, tie(halo, kv12)
    )
    kv3 = tie(kv_of(three), squares)
    far3 = send(kv3, SIBLING)
    total = swap_sum(squares[0], 1, kv3)
    late = jnp.concatenate([kv3, far12])
    low3 = send(late, DOWN)
    low4 = send(kv3, ASLANT)
    core2 = send(late, CORE)
    got = [messages[0], one, two, three]
    first = [(False, 0), (False, 1), (False, 2), (True, 0)]
    second = [(False, 3), (True, 1), (True, 2)]
    third = [(True, 3)]
    state = wave(
        got,
        [got[0], got[1], got[2], far0, core1],
        [block(n, ROWS, False, False, n, False) for n in range(3)]
        + group(3, [(True, 0)], False, False)
        + group(4, first, False, True),
        None,
    )
    far3 = tie(far3, state[1])
    core3 = send(jnp.concatenate([far3, low0, low12]), CORE)
    total = swap_sum(total, 2, state[1])
    state = wave(
        got,
        [got[3], far12, tie(core2, total), far3, low0, low12],
        [block(0, ROWS, False, False, 3, False)]
        + group(1, second[1:], False, False)
        + group(2, second, False, True)
        + group(3, third, False, False)
        + group(4, first[:1], True, False)
        + group(5, first[1:], True, False),
        state,
    )
    low3 = tie(low3, state[1])
    core4 = send(jnp.concatenate([low3, low4]), CORE)
    state = wave(
        got,
        [core3],
        group(0, third, False, True) + group(0, first, True, True, 2 * ROWS),
        state,
    )
    pieces = wave(
        got,
        [low3, low4, core4],
        group(0, second, True, False)
        + group(1, third, True, False)
        + group(2, second + third, True, True),
        state,
        last=True,
    )
    total = swap_sum(total, 4, pieces[0])
    returning = [back(pieces[j], NEAR[j]) for j in (3, 2, 1)]
    returned = [pieces[0]] + returning[::-1]
    heads_out = unpack(returned)

    mean_square = total[:, None] / D
    normed = (
        residual_out.astype(F32) * lax.rsqrt(mean_square + 1e-06) * norm_gain[None, :]
    ).astype(BF16)
    return (residual_out, normed, heads_out)


def solution(mesh):
    split_both = P("context", "tensor")
    return jax.shard_map(
        local,
        mesh=mesh,
        in_specs=(
            split_both,
            split_both,
            split_both,
            P("tensor", None),
            split_both,
            P("tensor"),
            split_both,
            split_both,
            split_both,
        ),
        out_specs=(split_both, split_both, split_both),
        check_vma=False,
    )
```

```python
import functools
import math

import jax
import jax.numpy as jnp
import ml_dtypes
import numpy as np
from jax import lax
from jax.experimental import pallas as pl
from jax.experimental.pallas import tpu as pltpu
from jax.sharding import PartitionSpec as P

D = 8192
DH = 128
ROWS = 256
TAPS = 128
SPAN = 2 * TAPS
ZS = 8
LOG2E_SCALE = math.log2(math.e) / math.sqrt(DH)
LOW = -1e30
F32 = jnp.float32
BF16 = jnp.bfloat16


def pairs(where):
    out = []
    for plane in range(2):
        for z in range(ZS):
            for core in range(2):
                to = where(plane, z, core)
                if to is not None:
                    p, zz, c = to
                    out.append(((plane * ZS + z) * 2 + core, (p * ZS + zz % ZS) * 2 + c))
    return out


def hop(steps):
    return pairs(lambda p, z, c: (p, z + steps[z % 2], c))


NEAR = [None, hop((-1, 1)), hop((2, -2)), hop((-3, 3))]
SIBLING = pairs(lambda p, z, c: (p, z ^ 1, c))
CORE = pairs(lambda p, z, c: (p, z, 1 - c))
DOWN = pairs(lambda p, z, c: (1, z, c) if p == 0 else None)
ASLANT = pairs(lambda p, z, c: (1, z ^ 1, c) if p == 0 else None)
NEXT = [(i, i + 1) for i in range(2 * ZS * 2 - 1)]


def send(x, where):
    return lax.ppermute(x, "context", where)


def back(x, where):
    return lax.ppermute(x, "context", [(b, a) for a, b in where])


def place():
    index = lax.axis_index("context")
    core = lax.rem(index, 2)
    z = lax.rem(lax.div(index, 2), ZS)
    plane = lax.div(index, 2 * ZS)
    return plane, z, core


def target_heads(z):
    odd = lax.rem(z, 2)
    offsets = [0, -1 + 2 * odd, 2 - 4 * odd, -3 + 6 * odd]
    return [lax.div(lax.rem(z + o + ZS, ZS), 2) for o in offsets]


def column_copies(refs, out, head, sems):
    columns = pl.ds(pl.multiple_of(head * DH, DH), DH)
    return [
        pltpu.make_async_copy(ref.at[:, columns], out.at[n * ROWS : (n + 1) * ROWS, :], sems.at[n])
        for n, ref in enumerate(refs)
    ]


def pack_kernel(q_ref, k_ref, v_ref, o1, o2, sems):
    heads = target_heads(place()[1])
    copies = []
    for n, (j, out) in enumerate(((1, o1), (2, o2))):
        copies += column_copies((q_ref, k_ref, v_ref), out, heads[j], sems.at[n])
    for copy in copies:
        copy.start()
    for copy in copies:
        copy.wait()


def pack_rest_kernel(
    q_ref, k_ref, v_ref, key_ref, value_ref, edge, o0, o3, own, key_tail, value_tail, sems
):
    heads = target_heads(place()[1])
    tails = [
        pltpu.make_async_copy(ref.at[ROWS - TAPS : ROWS, :], tail, sems.at[3, n])
        for n, (ref, tail) in enumerate(((key_ref, key_tail), (value_ref, value_tail)))
    ]
    copies = column_copies((k_ref, v_ref), own, heads[0], sems.at[0])
    for n, (j, out) in enumerate(((0, o0), (3, o3))):
        copies += column_copies((q_ref, k_ref, v_ref), out, heads[j], sems.at[1 + n])
    for copy in copies + tails:
        copy.start()
    for copy in tails:
        copy.wait()
    edge[...] = (key_tail[...].astype(F32) * value_tail[...].astype(F32)).astype(BF16)
    for copy in copies:
        copy.wait()


def pack(q, k, v):
    return pl.pallas_call(
        pack_kernel,
        out_shape=[jax.ShapeDtypeStruct((3 * ROWS, DH), BF16)] * 2,
        in_specs=[pl.BlockSpec(memory_space=pltpu.HBM)] * 3,
        out_specs=[pl.BlockSpec(memory_space=pltpu.VMEM)] * 2,
        scratch_shapes=[pltpu.SemaphoreType.DMA((2, 3))],
        compiler_params=pltpu.CompilerParams(vmem_limit_bytes=60 << 20),
        name="pack",
    )(q, k, v)


def pack_rest(q, k, v, key, value):
    channels = key.shape[1]
    return pl.pallas_call(
        pack_rest_kernel,
        out_shape=[jax.ShapeDtypeStruct((TAPS, channels), BF16)]
        + [jax.ShapeDtypeStruct((3 * ROWS, DH), BF16)] * 2
        + [jax.ShapeDtypeStruct((2 * ROWS, DH), BF16)],
        in_specs=[pl.BlockSpec(memory_space=pltpu.HBM)] * 5,
        out_specs=[pl.BlockSpec(memory_space=pltpu.VMEM)] * 4,
        scratch_shapes=[pltpu.VMEM((TAPS, channels), BF16)] * 2
        + [pltpu.SemaphoreType.DMA((4, 3))],
        compiler_params=pltpu.CompilerParams(vmem_limit_bytes=60 << 20),
        name="pack_rest",
    )(q, k, v, key, value)


def unpack_kernel(o0, o1, o2, o3, out):
    _, z, _ = place()
    for head, piece in zip(target_heads(z), (o0, o1, o2, o3)):
        out[:, pl.ds(pl.multiple_of(head * DH, DH), DH)] = piece[...]


def unpack(pieces):
    return pl.pallas_call(
        unpack_kernel,
        out_shape=jax.ShapeDtypeStruct((ROWS, 4 * DH), BF16),
        in_specs=[pl.BlockSpec(memory_space=pltpu.VMEM)] * 4,
        out_specs=pl.BlockSpec(memory_space=pltpu.VMEM),
        compiler_params=pltpu.CompilerParams(vmem_limit_bytes=16 << 20),
        name="unpack",
    )(*pieces)


def wave_kernel(blocks, first, last, count, *refs):
    q_refs = refs[:4]
    array_refs = refs[4 : 4 + count]
    rest = refs[4 + count :]
    if not first:
        acc_in, high_in = rest[:2]
        rest = rest[2:]
    if last:
        outs = rest[:4]
        rest = rest[4:]
    else:
        acc, high = rest[:2]
        rest = rest[2:]
    s_all, values_all = rest
    plane, z, core = place()
    odd = lax.rem(z, 2)
    sign = 2 * odd - 1
    skew = lax.broadcasted_iota(jnp.int32, (ROWS, ROWS), 1) - lax.broadcasted_iota(
        jnp.int32, (ROWS, ROWS), 0
    )
    values_all[:, DH:] = jnp.ones((values_all.shape[0], DH), BF16)

    def source(far, j):
        if far:
            return lax.rem((z + 1 - 2 * odd) - sign * j + ZS, ZS)
        return lax.rem(z + sign * j + ZS, ZS)

    def run(chosen):
        width = len(chosen) * ROWS
        for n, (array, k_row, v_row, lower, far, j, other) in enumerate(chosen):
            values_all[n * ROWS : (n + 1) * ROWS, :DH] = array_refs[array][v_row : v_row + ROWS, :]

        def scores(i):
            q = q_refs[i][0:ROWS, :]
            q_block = 2 * lax.rem(z + sign * i + ZS, ZS) + core
            old = None if first else high_in[i * ROWS : (i + 1) * ROWS, :]
            top = old
            for n, (array, k_row, v_row, lower, far, j, other) in enumerate(chosen):
                keys = array_refs[array][k_row : k_row + ROWS, :]
                s = lax.dot_general(
                    q, keys, (((1,), (1,)), ((), ())), preferred_element_type=F32
                )
                if not lower:
                    k_block = 2 * source(far, j) + (1 - core if other else core)
                    s = jnp.where(skew <= (q_block - k_block) * ROWS, s, LOW)
                s_all[i % 2, :, n * ROWS : (n + 1) * ROWS] = s
                pair = jnp.maximum(s[:, :DH], s[:, DH:])
                top = pair if top is None else jnp.maximum(top, pair)
            best = jnp.max(top, axis=1, keepdims=True)
            scale = None if first else jnp.exp2((old[:, :1] - best) * LOG2E_SCALE)
            return best, scale

        def weigh(i, best, scale):
            rows = slice(i * ROWS, (i + 1) * ROWS)
            p = jnp.exp2((s_all[i % 2, :, :width] - best) * LOG2E_SCALE).astype(BF16)
            total = jnp.dot(p, values_all[:width, :], preferred_element_type=F32)
            if not first:
                total = total + acc_in[rows, :] * scale
            if last:
                outs[i][...] = (total[:, :DH] / total[:, DH:]).astype(BF16)
            else:
                acc[rows, :] = total
                high[rows, :] = jnp.broadcast_to(best, (ROWS, DH))

        state = scores(0)
        for i in range(4):
            following = scores(i + 1) if i < 3 else None
            weigh(i, *state)
            state = following

    def keep():
        if last:
            for i in range(4):
                part = acc_in[i * ROWS : (i + 1) * ROWS, :]
                outs[i][...] = (part[:, :DH] / part[:, DH:]).astype(BF16)
        else:
            acc[...] = acc_in[...]
            high[...] = high_in[...]

    own = [b for b in blocks if not b[3]]
    if len(own) == len(blocks):
        run(own)
    else:

        @pl.when(plane == 1)
        def _():
            run(blocks)

        @pl.when(plane == 0)
        def _():
            if own:
                run(own)
            else:
                keep()


SMALL = pl.CostEstimate(flops=1024, bytes_accessed=1024, transcendentals=0)


def wave(q_arrays, arrays, blocks, state, last=False):
    first = state is None
    width = len(blocks) * ROWS
    state_shapes = [((4 * ROWS, 2 * DH), F32), ((4 * ROWS, DH), F32)]
    vmem = pl.BlockSpec(memory_space=pltpu.VMEM)
    if last:
        out_shape = [jax.ShapeDtypeStruct((ROWS, DH), BF16)] * 4
    else:
        out_shape = [jax.ShapeDtypeStruct(s, d) for s, d in state_shapes]
    operands = list(q_arrays) + list(arrays) + ([] if first else list(state))
    tiles = 4 * len(blocks)
    return pl.pallas_call(
        functools.partial(wave_kernel, blocks, first, last, len(arrays)),
        out_shape=out_shape,
        in_specs=[vmem] * len(operands),
        out_specs=[vmem] * len(out_shape),
        scratch_shapes=[
            pltpu.VMEM((2, ROWS, width), F32),
            pltpu.VMEM((width, 2 * DH), BF16),
        ],
        compiler_params=pltpu.CompilerParams(vmem_limit_bytes=32 << 20),
        cost_estimate=SMALL,
        name="wave",
    )(*operands)


def tie(x, *before):
    return lax.optimization_barrier((x,) + before)[0]


def kv_of(message):
    return message[ROWS:]


def tie(x, *before):
    return lax.optimization_barrier((x,) + before)[0]


def block(array, first_row, lower, far, j, other):
    return (array, first_row, first_row + ROWS, lower, far, j, other)


def group(array, spots, lower, other, skip=0):
    return [
        block(array, skip + 2 * ROWS * n, lower, far, j, other) for n, (far, j) in enumerate(spots)
    ]


def split(x):
    top = x.astype(BF16)
    return top, (x - top.astype(F32)).astype(BF16)


def transform():
    k = np.arange(SPAN // 2)[:, None] + 0.5
    t = np.arange(SPAN)[None, :]
    angle = 2 * np.pi * k * t / SPAN
    forward = np.concatenate([np.cos(angle), np.sin(angle)], axis=0)
    inverse = forward[:, TAPS:].T * (2.0 / SPAN)

    def halves(a):
        top = a.astype(ml_dtypes.bfloat16)
        return [top, (a - top.astype(np.float64)).astype(ml_dtypes.bfloat16)]

    return np.concatenate(
        [np.concatenate(halves(forward), axis=1), np.concatenate(halves(inverse), axis=1)], axis=0
    )


def filter_kernel(
    tile, matrix_ref, key_ref, value_ref, gate_ref, res_ref, taps_ref, halo_ref, out_ref, squares_ref
):
    def dot(a, b):
        return jnp.dot(a, b, preferred_element_type=F32)

    def dot_t(a, b):
        return lax.dot_general(a, b, (((1,), (1,)), ((), ())), preferred_element_type=F32)

    half = SPAN // 2
    forward, inverse = matrix_ref[:SPAN, :], matrix_ref[SPAN:, :]
    on_taps = jnp.concatenate([forward[:, :TAPS], forward[:, SPAN : SPAN + TAPS]], axis=1)
    squares = jnp.zeros((ROWS, tile), F32)
    for first in range(0, key_ref.shape[1], tile):
        columns = slice(first, first + tile)
        gated = (key_ref[:, columns].astype(F32) * value_ref[:, columns].astype(F32)).astype(BF16)
        x = jnp.concatenate(
            [jnp.concatenate([halo_ref[:, columns], gated[:TAPS]], axis=0), gated], axis=1
        )
        spectrum = dot(forward, jnp.concatenate([x, x], axis=0))
        taps = taps_ref[columns, :]
        weight = dot_t(on_taps, jnp.concatenate([taps, taps], axis=1))
        xc, xs = spectrum[:half], spectrum[half:]
        wc, ws = [jnp.concatenate([w, w], axis=1) for w in (weight[:half], weight[half:])]
        both = jnp.concatenate([xc * wc - xs * ws, xc * ws + xs * wc], axis=0)
        top, low = split(both)
        filtered = dot(inverse, jnp.concatenate([top, top], axis=0)) + dot(inverse[:, :SPAN], low)
        filtered = jnp.concatenate([filtered[:, :tile], filtered[:, tile:]], axis=0)
        out = (
            res_ref[:, columns].astype(F32) + gate_ref[:, columns].astype(F32) * filtered
        ).astype(BF16)
        out_ref[:, columns] = out
        wide = out.astype(F32)
        squares = squares + wide * wide
    top, low = split(squares)
    ones = jnp.ones((8, tile), BF16)
    squares_ref[...] = dot_t(ones, top) + dot_t(ones, low)


def filter_block(gate, key, value, filters, residual, halo):
    channels = gate.shape[1]
    vmem = pl.BlockSpec(memory_space=pltpu.VMEM)
    return pl.pallas_call(
        functools.partial(filter_kernel, 256),
        out_shape=[
            jax.ShapeDtypeStruct((ROWS, channels), BF16),
            jax.ShapeDtypeStruct((8, ROWS), F32),
        ],
        in_specs=[vmem] * 7,
        out_specs=[vmem] * 2,
        compiler_params=pltpu.CompilerParams(vmem_limit_bytes=32 << 20),
        cost_estimate=SMALL,
        name="filter",
    )(jnp.asarray(transform()), key, value, gate, residual, filters, halo)


def swap_sum(x, bit, *before):
    return lax.ppermute(x, "tensor", [(i, i ^ bit) for i in range(8)]) + tie(x, *before)


def local(
    gate_proj,
    key_proj,
    value_proj,
    filters,
    residual_in,
    norm_gain,
    queries,
    attn_keys,
    attn_values,
):
    message1, message2 = pack(queries, attn_keys, attn_values)
    one = send(message1, NEAR[1])
    two = send(message2, NEAR[2])
    edge, message0, message3, kv0 = pack_rest(
        tie(queries, message1), attn_keys, attn_values, key_proj, value_proj
    )
    messages = [message0, message1, message2, message3]
    far0 = send(kv0, SIBLING)
    low0 = send(kv0, DOWN)
    halo = send(edge, NEXT)

    three = send(tie(messages[3], one), NEAR[3])
    kv12 = tie(jnp.concatenate([kv_of(one), kv_of(two)]), far0, low0)
    far12 = send(kv12, SIBLING)
    mid = jnp.concatenate([kv12, far0])
    low12 = send(mid, DOWN)
    core1 = send(jnp.concatenate([kv0, mid]), CORE)

    gate_proj, key_proj, value_proj, filters, residual_in, _ = lax.optimization_barrier(
        (gate_proj, key_proj, value_proj, filters, residual_in, messages[0])
    )
    residual_out, squares = filter_block(
        gate_proj, key_proj, value_proj, filters, residual_in, tie(halo, kv12)
    )
    kv3 = tie(kv_of(three), squares)
    far3 = send(kv3, SIBLING)
    total = swap_sum(squares[0], 1, kv3)
    late = jnp.concatenate([kv3, far12])
    low3 = send(late, DOWN)
    low4 = send(kv3, ASLANT)
    core2 = send(late, CORE)
    got = [messages[0], one, two, three]
    first = [(False, 0), (False, 1), (False, 2), (True, 0)]
    second = [(False, 3), (True, 1), (True, 2)]
    third = [(True, 3)]
    state = wave(
        got,
        [got[0], got[1], got[2], far0, core1],
        [block(n, ROWS, False, False, n, False) for n in range(3)]
        + group(3, [(True, 0)], False, False)
        + group(4, first, False, True),
        None,
    )
    far3 = tie(far3, state[1])
    core3 = send(jnp.concatenate([far3, low0, low12]), CORE)
    state = wave(
        got,
        [got[3], far12, tie(core2, total), far3, low0, low12],
        [block(0, ROWS, False, False, 3, False)]
        + group(1, second[1:], False, False)
        + group(2, second, False, True)
        + group(3, third, False, False)
        + group(4, first[:1], True, False)
        + group(5, first[1:], True, False),
        state,
    )
    total = swap_sum(total, 2, state[1])
    low3 = tie(low3, state[1], total)
    core4 = send(jnp.concatenate([low3, low4]), CORE)
    state = wave(
        got,
        [core3],
        group(0, third, False, True) + group(0, first, True, True, 2 * ROWS),
        state,
    )
    pieces = wave(
        got,
        [low3, low4, core4],
        group(0, second, True, False)
        + group(1, third, True, False)
        + group(2, second + third, True, True),
        state,
        last=True,
    )
    total = swap_sum(total, 4, pieces[0])
    returning = [back(pieces[j], NEAR[j]) for j in (3, 2, 1)]
    returned = [pieces[0]] + returning[::-1]
    heads_out = unpack(returned)

    mean_square = total[:, None] / D
    normed = (
        residual_out.astype(F32) * lax.rsqrt(mean_square + 1e-06) * norm_gain[None, :]
    ).astype(BF16)
    return (residual_out, normed, heads_out)


def solution(mesh):
    split_both = P("context", "tensor")
    return jax.shard_map(
        local,
        mesh=mesh,
        in_specs=(
            split_both,
            split_both,
            split_both,
            P("tensor", None),
            split_both,
            P("tensor"),
            split_both,
            split_both,
            split_both,
        ),
        out_specs=(split_both, split_both, split_both),
        check_vma=False,
    )
```
